32 devices in a mesh: rep: 2 (over x), blk: 8 (over z, y), width: 2 (over core).
Axes of the slice: x: 2, y: 2, z: 4, core: 2. Of those that a mesh axis runs over, the one named last changes fastest.
Arguments:
- tokens: bfloat16 [256, 16384], P(('rep', 'blk'), 'width'), parts along dimension 0, may hold values from -6 to 6
- norm_gain: float32 [16384], P('width'), as said below
- w_query: bfloat16 [16384, 8192], P('width', 'blk'), may hold values from -0.046875 to 0.046875
- w_key: bfloat16 [16384, 512], P('width', 'blk'), may hold values from -0.046875 to 0.046875
- w_value: bfloat16 [16384, 512], P('width', 'blk'), may hold values from -0.046875 to 0.046875
- w_output: bfloat16 [8192, 16384], P('blk', 'width'), may hold values from -0.0625 to 0.0625
- seq_ids: int32 [256], P('rep'), parts along dimension 0, may hold values from 0 to 7, never falling along the last dimension, each value on 1 to 32 neighbouring positions
Outputs:
- attended: bfloat16 [256, 16384], P(('rep', 'blk'), 'width'), parts along dimension 0
The draws below stay inside these ranges and needn't reach their ends.
There are 2 independent parts, one for each index of `rep`. The reference program is written for one: setup_inputs(seed, part) draws one part's arguments, and reference() takes and returns one part's arrays. A program takes and returns all parts, laid end to end along the dimension named above; an argument that names none is the same for every part. Nothing has to cross between parts.
Inputs may be any that keep to these rules, and one draw needn't show every extreme that they name: `norm_gain`: Positive. `seq_ids`: never falling; each of the 8 sequences holds consecutive tokens, 1 to 32 of them, and one holds exactly 32.
All inputs are finite; a program needn't handle non-finite values.
Results may differ from the reference program's by a relative error of at most 0.035.
Values may be sent and summed in bfloat16 or wider, within the bound.
A program may use at most 128 MiB of HBM per device.

```python
import math
import jax
import jax.numpy as jnp
import numpy as np
from jax import lax

D = 16384
HEADS = 64
KV_HEADS = 4
HEAD = 128
SEQS = 8
TOKENS = 128
SEQ_MAX = 32
N_BLK = 8


def draw_norm_gain(key, part):
    key = jax.random.fold_in(key, 11)
    return jax.random.uniform(key, (D,), jnp.float32, 0.6, 1.6)


def levels(own_key, shape, split, smallest, top_value):
    def one(dim, parts):
        steps = jax.random.uniform(jax.random.fold_in(jax.random.fold_in(own_key, 6), dim), (parts,), jnp.float32, smallest / len(split), top_value / len(split))
        return jnp.repeat(jnp.exp(steps), shape[dim] // parts).reshape((-1,) + (1,) * (len(shape) - dim - 1))

    factor_of = one(*split[0])
    for cut in split[1:]:
        factor_of = factor_of * one(*cut)
    return factor_of


def length_profile(count, total, reach, lean):
    portions = [(1 << 20) // math.isqrt(grade ** lean) + 1 for grade in range(2, count + 1)]
    spare, given = total - reach - (count - 1), [1] * (count - 1)
    while spare > 0:
        free = [i for i in range(count - 1) if given[i] < reach]
        pool, left = sum([portions[i] for i in free]), spare
        for i in free:
            extra = min(reach - given[i], max(1, left * portions[i] // pool), spare)
            given[i] = given[i] + extra
            spare = spare - extra
    return np.array([reach] + given)


def ragged(key, count, total, most, skew):
    if count == 2:
        one = jax.random.randint(key, (), max(1, total - most), min(most, total - 1) + 1)
        return jnp.stack([one, total - one])
    sizes = jnp.asarray(length_profile(count, total, most, skew), jnp.int32)
    pairs = (count - 1) // 2
    source_of, sink = sizes[1:1 + 2 * pairs:2], sizes[2:2 + 2 * pairs:2]
    room = jnp.minimum(source_of - 1, most - sink)
    passed = jax.random.randint(jax.random.fold_in(key, 1), (pairs,), 0, 1 << 20) % (room + 1)
    sizes = sizes.at[1:1 + 2 * pairs:2].set(source_of - passed).at[2:2 + 2 * pairs:2].set(sink + passed)
    return sizes[jax.random.permutation(jax.random.fold_in(key, 2), count)]


def bell_draw(own_key, extent, deviation, bound, shards=(), kind=jnp.bfloat16):
    level = levels(own_key, extent, shards, -0.22, 0.18) if shards else 1.0
    result = jax.random.normal(own_key, extent, jnp.float32) * deviation * level
    return jnp.minimum(jnp.maximum(result, -bound), bound).astype(kind)


def setup_inputs(seed: int = 0, part: int = 0) -> dict:
    key_list = jax.random.split(jax.random.key(seed), 8)
    own_keys = jax.random.split(jax.random.fold_in(key_list[7], part), 8)
    tokens = bell_draw(own_keys[0], (TOKENS, D), 1.0, 6.0, ((0, 8), (1, 2)))
    norm_gain = draw_norm_gain(jax.random.fold_in(key_list[7], 71), part)
    w_query = bell_draw(key_list[2], (D, HEADS * HEAD), D ** -0.5, 0.046875, ((0, 2), (1, 8)))
    w_key = bell_draw(key_list[3], (D, KV_HEADS * HEAD), D ** -0.5, 0.046875, ((0, 2), (1, 8)))
    w_value = bell_draw(key_list[4], (D, KV_HEADS * HEAD), D ** -0.5, 0.046875, ((0, 2), (1, 8)))
    w_output = bell_draw(key_list[5], (HEADS * HEAD, D), (HEADS * HEAD) ** -0.5, 0.0625, ((0, 8), (1, 2)))
    seq_ids = jnp.searchsorted(jnp.cumsum(ragged(own_keys[6], SEQS, TOKENS, SEQ_MAX, 1)), jnp.arange(TOKENS), side="right").astype(jnp.int32)
    return dict(tokens=tokens, norm_gain=norm_gain, w_query=w_query, w_key=w_key, w_value=w_value, w_output=w_output, seq_ids=seq_ids)


EPSILON = 1e-05

def rotate(values_in, positions):
    half_dim = values_in.shape[-1] // 2
    freqs = 500000.0 ** (-2.0 * jnp.arange(half_dim, dtype=jnp.float32) / values_in.shape[-1])
    angles = positions.astype(jnp.float32)[:, None] * freqs[None, :]
    cosine = jnp.cos(angles)[:, None, :]
    sine = jnp.sin(angles)[:, None, :]
    lower = values_in[..., :half_dim]
    upper = values_in[..., half_dim:]
    return jnp.concatenate([lower * cosine - upper * sine, upper * cosine + lower * sine], axis=-1)

def reference(tokens, norm_gain, w_query, w_key, w_value, w_output, seq_ids):
    floats = tokens.astype(jnp.float32)
    mean_square = lax.optimization_barrier(jnp.mean(floats * floats, axis=1))
    normed = (floats * lax.rsqrt(mean_square + EPSILON)[:, None] * norm_gain[None, :]).astype(jnp.bfloat16)
    index_row = jnp.arange(TOKENS, dtype=jnp.int32)
    starts = lax.optimization_barrier(jnp.sum((seq_ids[None, :] < seq_ids[:, None]).astype(jnp.int32), axis=1))
    positions = index_row - starts
    q_raw = jnp.dot(normed, w_query, preferred_element_type=jnp.float32)
    k_raw = jnp.dot(normed, w_key, preferred_element_type=jnp.float32)
    v_raw = jnp.dot(normed, w_value, preferred_element_type=jnp.float32)
    k_heads = jnp.transpose(k_raw.reshape(TOKENS, HEAD, KV_HEADS), (0, 2, 1))
    v_heads = jnp.transpose(v_raw.reshape(TOKENS, HEAD, KV_HEADS), (0, 2, 1))
    queries = rotate(q_raw.reshape(TOKENS, HEADS, HEAD), positions).astype(jnp.bfloat16)
    keys_rot = rotate(k_heads, positions).astype(jnp.bfloat16)
    values_bf = v_heads.astype(jnp.bfloat16)
    group = HEADS // KV_HEADS
    grouped = queries.astype(jnp.float32).reshape(TOKENS, KV_HEADS, group, HEAD)
    scores = jnp.einsum('tkgd,skd->kgts', grouped, keys_rot.astype(jnp.float32)) / jnp.sqrt(jnp.float32(HEAD))
    allowed = (seq_ids[None, :] == seq_ids[:, None]) & (index_row[None, :] <= index_row[:, None])
    scores = jnp.where(allowed[None, None], scores, jnp.float32(-jnp.inf))
    row_top = lax.optimization_barrier(jnp.max(scores, axis=-1, keepdims=True))
    raised = jnp.exp(scores - row_top)
    probs = (raised / lax.optimization_barrier(jnp.sum(raised, axis=-1, keepdims=True))).astype(jnp.bfloat16)
    context = jnp.einsum('kgts,skd->tkgd', probs.astype(jnp.float32), values_bf.astype(jnp.float32))
    context = context.astype(jnp.bfloat16).reshape(TOKENS, HEADS * HEAD)
    group_rows = HEADS * HEAD // N_BLK
    context_groups = jnp.transpose(context.reshape(TOKENS, N_BLK, group_rows), (1, 0, 2))
    weight_groups = w_output.reshape(N_BLK, group_rows, D)

    def add_group(total, pair):
        term = jnp.dot(pair[0], pair[1], preferred_element_type=jnp.float32).astype(jnp.bfloat16)
        term = lax.optimization_barrier(term)
        return (total + term.astype(jnp.float32), None)
    summed, unused = lax.scan(add_group, jnp.zeros((TOKENS, D), jnp.float32), (context_groups, weight_groups))
    return summed.astype(jnp.bfloat16)
```

```python
import functools
import math

import jax
import jax.numpy as jnp
from jax import lax
from jax.experimental import pallas as pl
from jax.experimental.pallas import tpu as pltpu
from jax.sharding import PartitionSpec as P

HEADS = 64
KV_HEADS = 4
HEAD = 128

EPSILON = 1e-05
THETA = 500000.0

NZ = 4
NY = 2
WIDTH = 2
CHUNKS = 4
TILE = 512

NT = (((1,), (1,)), ((), ()))


def rotate(values_in, positions):
    half_dim = values_in.shape[-1] // 2
    freqs = THETA ** (-2.0 * jnp.arange(half_dim, dtype=jnp.float32) / values_in.shape[-1])
    angles = positions.astype(jnp.float32)[:, None] * freqs[None, :]
    cosine = jnp.cos(angles)[:, None, :]
    sine = jnp.sin(angles)[:, None, :]
    lower = values_in[..., :half_dim]
    upper = values_in[..., half_dim:]
    return jnp.concatenate([lower * cosine - upper * sine, upper * cosine + lower * sine], axis=-1)


def collective_form(tokens, norm_gain, w_query, w_key, w_value, w_output, seq_ids):
    rows_blk, half_width = tokens.shape
    width_full = half_width * lax.axis_size("width")
    total_rows = rows_blk * lax.axis_size("blk")
    floats = tokens.astype(jnp.float32)
    row_squares = lax.psum(jnp.sum(floats * floats, axis=1), "width")
    normed = (
        floats * lax.rsqrt(row_squares / width_full + EPSILON)[:, None] * norm_gain[None, :]
    ).astype(jnp.bfloat16)
    query_cols = w_query.shape[1]
    kv_width = w_key.shape[1]
    weights_all = jnp.concatenate([w_query, w_key, w_value], axis=1)
    partial_sums = jnp.dot(
        lax.all_gather(normed, "blk", axis=0, tiled=True),
        weights_all,
        preferred_element_type=jnp.float32,
    )
    summed = lax.psum(partial_sums, "width")
    q_raw = summed[:, :query_cols]
    kv_raw = summed[:, query_cols:]
    query_rows = q_raw.shape[0]
    stacked = jnp.stack([kv_raw[:, :kv_width], kv_raw[:, kv_width:]])
    every_kv = lax.all_gather(stacked.astype(jnp.bfloat16), "blk", axis=2, tiled=True).astype(
        stacked.dtype
    )
    heads_dev = query_cols // HEAD
    group = HEADS // KV_HEADS
    kv_index = lax.axis_index("blk") * heads_dev // group
    split_heads = every_kv.reshape(2, total_rows, HEAD, KV_HEADS)
    own_head = lax.dynamic_index_in_dim(split_heads, kv_index, 3, keepdims=False)
    keys_raw = own_head[0]
    values_raw = own_head[1]
    index_row = jnp.arange(total_rows, dtype=jnp.int32)
    starts = jnp.sum((seq_ids[None, :] < seq_ids[:, None]).astype(jnp.int32), axis=1)
    positions = index_row - starts
    queries = rotate(q_raw.reshape(query_rows, heads_dev, HEAD), positions).astype(jnp.bfloat16)
    keys_rot = rotate(keys_raw[:, None, :], positions)[:, 0, :].astype(jnp.bfloat16)
    values_bf = values_raw.astype(jnp.bfloat16)
    scores = jnp.einsum(
        "thd,sd->hts", queries, keys_rot, preferred_element_type=jnp.float32
    ) / jnp.sqrt(jnp.float32(HEAD))
    allowed = (seq_ids[None, :] == seq_ids[:, None]) & (index_row[None, :] <= index_row[:, None])
    scores = jnp.where(allowed[None], scores, jnp.float32(-jnp.inf))
    row_top = jnp.max(scores, axis=-1, keepdims=True)
    raised = jnp.exp(scores - row_top)
    probs = (raised / jnp.sum(raised, axis=-1, keepdims=True)).astype(jnp.bfloat16)
    context = jnp.einsum("hts,sd->thd", probs, values_bf, preferred_element_type=jnp.float32)
    context = context.astype(jnp.bfloat16).reshape(query_rows, query_cols)
    complete = lax.psum(
        jnp.dot(context, w_output, preferred_element_type=jnp.float32).astype(jnp.bfloat16), "blk"
    ).astype(jnp.float32)
    result = lax.dynamic_slice_in_dim(complete, lax.axis_index("blk") * rows_blk, rows_blk, 0)
    return result.astype(jnp.bfloat16)


def fused_kernel(
    tok, gain, wq_hbm, wk_hbm, wv_hbm, wo_hbm, seq, out,
    wq, wk, wv, wo, xg, acc_q, acc_kv, acc_ss, q_send, q_recv, ss_send, ss_recv,
    kv_send, kv_recv, cos_q, sin_q, cos_k, sin_k, bias, ctx, part, y_part, summed, z_part,
    w_sem, wo_sem, kvw_sem, gz_send, gz_recv, gy_send, gy_recv,
    ex_send, ex_recv, kv_ssem, kv_rsem, ry_send, ry_recv, rz_send, rz_recv,
):
    rows, width = tok.shape
    n = NZ * NY
    total = rows * n
    cols = wq.shape[1]
    heads_dev = cols // HEAD
    kvw = wk.shape[1]
    per_head = kvw // KV_HEADS
    span = width // CHUNKS
    tile = min(TILE, span)
    half = HEAD // 2
    f32, bf16 = jnp.float32, jnp.bfloat16

    me = lax.axis_index("blk")
    core = lax.axis_index("width")
    y = me % NY
    z = me // NY
    other = 1 - core
    y_peer = z * NY + (1 - y)

    def chunk(c):
        return pl.ds(c * span, span)

    def z_blk(step):
        return ((z + step) % NZ) * NY + y

    wq_copies = [
        pltpu.make_async_copy(wq_hbm.at[chunk(c), :], wq.at[chunk(c), :], w_sem.at[c])
        for c in range(CHUNKS)
    ]
    wo_copies = [
        pltpu.make_async_copy(wo_hbm.at[:, chunk(c)], wo.at[:, chunk(c)], wo_sem.at[c])
        for c in range(CHUNKS)
    ]
    wk_copy = pltpu.make_async_copy(wk_hbm, wk, kvw_sem.at[0])
    wv_copy = pltpu.make_async_copy(wv_hbm, wv, kvw_sem.at[1])
    wk_copy.start()
    wv_copy.start()
    for copy in wq_copies + wo_copies:
        copy.start()

    barrier = pltpu.get_barrier_semaphore()
    for step in range(n):
        for side in range(WIDTH):
            if step == 0 and side == 0:
                continue
            pl.semaphore_signal(
                barrier, inc=1,
                device_id={"blk": (me + step) % n, "width": (core + side) % WIDTH},
                device_id_type=pl.DeviceIdType.MESH,
            )
    pl.semaphore_wait(barrier, n * WIDTH - 1)

    def remote(src, dst, s_sem, r_sem, blk, side):
        return pltpu.make_async_remote_copy(
            src_ref=src, dst_ref=dst, send_sem=s_sem, recv_sem=r_sem,
            device_id={"blk": blk, "width": side}, device_id_type=pl.DeviceIdType.MESH,
        )

    def gz(c, d, blk):
        return remote(tok.at[:, chunk(c)], xg.at[c, blk], gz_send.at[c, d - 1], gz_recv.at[c, d - 1], z_blk(d), core)

    def gy(c, d):
        src = tok.at[:, chunk(c)] if d == 0 else xg.at[c, z_blk(NZ - d)]
        return remote(src, xg.at[c, z_blk(NZ - d)], gy_send.at[c, d], gy_recv.at[c, d], y_peer, core)

    def gy_in(c, d):
        blk = ((z + NZ - d) % NZ) * NY + (1 - y)
        return remote(tok.at[:, chunk(c)], xg.at[c, blk], gy_send.at[c, d], gy_recv.at[c, d], y_peer, core)

    for c in range(CHUNKS):
        for d in range(1, NZ):
            gz(c, d, me).start()
        gy(c, 0).start()

    for c in range(CHUNKS):
        xg[c, me] = tok[:, c * span:(c + 1) * span]
    acc_q[...] = jnp.zeros_like(acc_q)
    acc_kv[...] = jnp.zeros_like(acc_kv)
    acc_ss[...] = jnp.zeros_like(acc_ss)
    by_col = jnp.broadcast_to(seq[...].astype(f32), (total, total))
    by_row = by_col.T
    at_row = lax.broadcasted_iota(jnp.int32, (total, total), 0)
    at_col = lax.broadcasted_iota(jnp.int32, (total, total), 1)
    starts_q = jnp.sum((by_col < by_row).astype(f32), axis=1, keepdims=True)
    starts_k = jnp.sum((by_row < by_col).astype(f32), axis=0, keepdims=True)
    bias[...] = jnp.where((by_col == by_row) & (at_col <= at_row), 0.0, -jnp.inf).astype(f32)
    rate = -2.0 * math.log(THETA) / HEAD
    lane = lax.broadcasted_iota(jnp.int32, (total, HEAD), 1)
    line = lax.broadcasted_iota(jnp.int32, (total, HEAD), 0)
    angle_q = (line.astype(f32) - starts_q) * jnp.exp((lane % half).astype(f32) * rate)
    cos_q[...] = jnp.cos(angle_q)
    sine = jnp.sin(angle_q)
    sin_q[...] = jnp.where(lane < half, -sine, sine)
    pos_k = lax.broadcasted_iota(jnp.int32, (half, total), 1).astype(f32) - starts_k
    angle_k = pos_k * jnp.exp(lax.broadcasted_iota(jnp.int32, (half, total), 0).astype(f32) * rate)
    cos_k[...] = jnp.cos(angle_k)
    sin_k[...] = jnp.sin(angle_k)

    def pass_on(c):
        for d in range(1, NZ):
            gz(c, d, z_blk(NZ - d)).wait_recv()
            gy(c, d).start()

    def project(c):
        def body(k, _):
            here = pl.ds(pl.multiple_of(k * tile, tile), tile)
            deep = pl.ds(pl.multiple_of(c * span + k * tile, tile), tile)
            x = xg[c, :, :, here].reshape(total, tile).astype(f32)
            squares = x * x
            folded = squares[:, :HEAD]
            for i in range(1, tile // HEAD):
                folded = folded + squares[:, i * HEAD:(i + 1) * HEAD]
            acc_ss[...] += folded
            scaled = (x * gain[:, deep]).astype(bf16)
            acc_q[...] += jnp.dot(scaled, wq[deep, :], preferred_element_type=f32)
            both = jnp.concatenate([wk[deep, :], wv[deep, :]], axis=1)
            acc_kv[...] += jnp.dot(scaled, both, preferred_element_type=f32)
            return 0

        lax.fori_loop(0, span // tile, body, 0)

    pass_on(0)
    for c in range(CHUNKS):
        if c + 1 < CHUNKS:
            pass_on(c + 1)
        for d in range(NZ):
            gy_in(c, d).wait_recv()
        if c == 0:
            wk_copy.wait()
            wv_copy.wait()
        wq_copies[c].wait()
        project(c)

    rr = lax.broadcasted_iota(jnp.int32, (2 * kvw, 2 * kvw), 0)
    cc = lax.broadcasted_iota(jnp.int32, (2 * kvw, 2 * kvw), 1)
    at = ((rr // per_head) % 2) * kvw + (rr % per_head) * KV_HEADS + rr // (2 * per_head)
    picks = jnp.where(cc == at, 1.0, 0.0).astype(bf16)
    turned = lax.dot_general(picks, acc_kv[...].astype(bf16), NT, preferred_element_type=f32)
    kv_send[...] = turned.astype(bf16).reshape(KV_HEADS, 2 * per_head, total)
    group = HEADS // KV_HEADS

    def kv_copy(step, side, blk, whose):
        to = (me + step) % n
        i = step * WIDTH + side
        return remote(
            kv_send.at[to * heads_dev // group], kv_recv.at[whose, blk],
            kv_ssem.at[i], kv_rsem.at[i], to, (core + side) % WIDTH,
        )

    pairs = [(s, side) for s in range(n) for side in range(WIDTH) if s or side]
    for s, side in pairs:
        kv_copy(s, side, me, core).start()
    kv_recv[core, me] = kv_send[me * heads_dev // group]
    ss_send[...] = jnp.broadcast_to(jnp.sum(acc_ss[...], axis=1, keepdims=True), (total, HEAD))
    ss_copy = remote(ss_send, ss_recv, ex_send.at[0], ex_recv.at[0], me, other)
    ss_copy.start()
    q_send[...] = acc_q[...].astype(bf16)
    q_copy = remote(q_send, q_recv, ex_send.at[1], ex_recv.at[1], me, other)
    q_copy.start()

    ss_copy.wait_recv()
    scale = lax.rsqrt((ss_send[...] + ss_recv[...]) / (WIDTH * width) + EPSILON)
    scale_k = scale.T
    q_copy.wait_recv()
    for s, side in pairs:
        kv_copy(s, side, (me + n - s) % n, (core + side) % WIDTH).wait_recv()
    kv = kv_recv[0].astype(f32) + kv_recv[1].astype(f32)
    keys = kv[:, :per_head].reshape(HEAD, total) * scale_k
    values = (kv[:, per_head:].reshape(HEAD, total) * scale_k).astype(bf16)
    low, high = keys[:half], keys[half:]
    keys = jnp.concatenate(
        [low * cos_k[...] - high * sin_k[...], high * cos_k[...] + low * sin_k[...]], axis=0
    ).astype(bf16)
    for h in range(heads_dev):
        own = slice(h * HEAD, (h + 1) * HEAD)
        q = (acc_q[:, own] + q_recv[:, own].astype(f32)) * scale
        q = (q * cos_q[...] + pltpu.roll(q, half, 1) * sin_q[...]).astype(bf16)
        scores = jnp.dot(q, keys, preferred_element_type=f32) * (1.0 / math.sqrt(HEAD)) + bias[...]
        raised = jnp.exp(scores - jnp.max(scores, axis=1, keepdims=True))
        probs = (raised / jnp.sum(raised, axis=1, keepdims=True)).astype(bf16)
        ctx[:, own] = lax.dot_general(probs, values, NT, preferred_element_type=f32).astype(bf16)

    def ry(c):
        return remote(part.at[c, 1 - y], y_part.at[c], ry_send.at[c], ry_recv.at[c], y_peer, core)

    def rz(c, d):
        return remote(
            summed.at[c, (z + d) % NZ], z_part.at[c, d - 1],
            rz_send.at[c, d - 1], rz_recv.at[c, d - 1], z_blk(d), core,
        )

    def multiply(c):
        wo_copies[c].wait()

        def body(k, _):
            here = pl.ds(pl.multiple_of(k * tile, tile), tile)
            deep = pl.ds(pl.multiple_of(c * span + k * tile, tile), tile)
            got = jnp.dot(ctx[...], wo[:, deep], preferred_element_type=f32).astype(bf16)
            got = got.reshape(NZ, NY, rows, tile)
            for i in range(NY):
                part[c, i, :, :, here] = got[:, i]
            return 0

        lax.fori_loop(0, span // tile, body, 0)
        ry(c).start()

    def add_y(c):
        ry(c).wait_recv()

        def body(k, _):
            here = pl.ds(pl.multiple_of(k * tile, tile), tile)
            summed[c, :, :, here] = (
                part[c, y, :, :, here].astype(f32) + y_part[c, :, :, here].astype(f32)
            ).astype(bf16)
            return 0

        lax.fori_loop(0, span // tile, body, 0)
        for d in range(1, NZ):
            rz(c, d).start()

    def add_z(c):
        for d in range(1, NZ):
            rz(c, d).wait_recv()
        found = summed[c, z].astype(f32)
        for d in range(1, NZ):
            found = found + z_part[c, d - 1].astype(f32)
        out[:, c * span:(c + 1) * span] = found.astype(bf16)

    for c in range(CHUNKS):
        multiply(c)
        if c > 0:
            add_y(c - 1)
    add_y(CHUNKS - 1)
    for c in range(CHUNKS):
        add_z(c)

    for c in range(CHUNKS):
        for d in range(1, NZ):
            gz(c, d, me).wait_send()
            rz(c, d).wait_send()
        for d in range(NZ):
            gy(c, d).wait_send()
        ry(c).wait_send()
    for s, side in pairs:
        kv_copy(s, side, me, core).wait_send()
    ss_copy.wait_send()
    q_copy.wait_send()


def kernel_form(tokens, norm_gain, w_query, w_key, w_value, w_output, seq_ids):
    rows, width = tokens.shape
    n = NZ * NY
    total = rows * n
    cols = w_query.shape[1]
    kvw = w_key.shape[1]
    per_head = kvw // KV_HEADS
    span = width // CHUNKS
    bf16, f32 = jnp.bfloat16, jnp.float32
    vmem = pl.BlockSpec(memory_space=pltpu.VMEM)
    hbm = pl.BlockSpec(memory_space=pl.ANY)
    dma = pltpu.SemaphoreType.DMA
    return pl.pallas_call(
        fused_kernel,
        out_shape=jax.ShapeDtypeStruct((rows, width), bf16),
        in_specs=[vmem, vmem, hbm, hbm, hbm, hbm, vmem],
        out_specs=vmem,
        scratch_shapes=[
            pltpu.VMEM((width, cols), bf16),
            pltpu.VMEM((width, kvw), bf16),
            pltpu.VMEM((width, kvw), bf16),
            pltpu.VMEM((cols, width), bf16),
            pltpu.VMEM((CHUNKS, n, rows, span), bf16),
            pltpu.VMEM((total, cols), f32),
            pltpu.VMEM((total, 2 * kvw), f32),
            pltpu.VMEM((total, HEAD), f32),
            pltpu.VMEM((total, cols), bf16),
            pltpu.VMEM((total, cols), bf16),
            pltpu.VMEM((total, HEAD), f32),
            pltpu.VMEM((total, HEAD), f32),
            pltpu.VMEM((KV_HEADS, 2 * per_head, total), bf16),
            pltpu.VMEM((WIDTH, n, 2 * per_head, total), bf16),
            pltpu.VMEM((total, HEAD), f32),
            pltpu.VMEM((total, HEAD), f32),
            pltpu.VMEM((HEAD // 2, total), f32),
            pltpu.VMEM((HEAD // 2, total), f32),
            pltpu.VMEM((total, total), f32),
            pltpu.VMEM((total, cols), bf16),
            pltpu.VMEM((CHUNKS, NY, NZ, rows, span), bf16),
            pltpu.VMEM((CHUNKS, NZ, rows, span), bf16),
            pltpu.VMEM((CHUNKS, NZ, rows, span), bf16),
            pltpu.VMEM((CHUNKS, NZ - 1, rows, span), bf16),
            dma((CHUNKS,)),
            dma((CHUNKS,)),
            dma((2,)),
            dma((CHUNKS, NZ - 1)),
            dma((CHUNKS, NZ - 1)),
            dma((CHUNKS, NZ)),
            dma((CHUNKS, NZ)),
            dma((2,)),
            dma((2,)),
            dma((n * WIDTH,)),
            dma((n * WIDTH,)),
            dma((CHUNKS,)),
            dma((CHUNKS,)),
            dma((CHUNKS, NZ - 1)),
            dma((CHUNKS, NZ - 1)),
        ],
        compiler_params=pltpu.CompilerParams(
            collective_id=0, has_side_effects=True, vmem_limit_bytes=60 * 1024 * 1024
        ),
        name="attention_block",
    )(
        tokens, norm_gain.reshape(1, width), w_query, w_key, w_value, w_output,
        seq_ids.reshape(1, total),
    )


def solution(mesh):
    placed = (
        P(("rep", "blk"), "width"),
        P("width"),
        P("width", "blk"),
        P("width", "blk"),
        P("width", "blk"),
        P("blk", "width"),
        P("rep"),
    )
    on_grid = mesh.shape["blk"] == NZ * NY and mesh.shape["width"] == WIDTH
    return jax.shard_map(
        kernel_form if on_grid else collective_form,
        mesh=mesh, in_specs=placed, out_specs=P(("rep", "blk"), "width"), check_vma=False,
    )
```

```python
import functools
import math

import jax
import jax.numpy as jnp
from jax import lax
from jax.experimental import pallas as pl
from jax.experimental.pallas import tpu as pltpu
from jax.sharding import PartitionSpec as P

HEADS = 64
KV_HEADS = 4
HEAD = 128

EPSILON = 1e-05
THETA = 500000.0

NZ = 4
NY = 2
WIDTH = 2
CHUNKS = 4
TILE = 1024

NT = (((1,), (1,)), ((), ()))


def rotate(values_in, positions):
    half_dim = values_in.shape[-1] // 2
    freqs = THETA ** (-2.0 * jnp.arange(half_dim, dtype=jnp.float32) / values_in.shape[-1])
    angles = positions.astype(jnp.float32)[:, None] * freqs[None, :]
    cosine = jnp.cos(angles)[:, None, :]
    sine = jnp.sin(angles)[:, None, :]
    lower = values_in[..., :half_dim]
    upper = values_in[..., half_dim:]
    return jnp.concatenate([lower * cosine - upper * sine, upper * cosine + lower * sine], axis=-1)


def collective_form(tokens, norm_gain, w_query, w_key, w_value, w_output, seq_ids):
    rows_blk, half_width = tokens.shape
    width_full = half_width * lax.axis_size("width")
    total_rows = rows_blk * lax.axis_size("blk")
    floats = tokens.astype(jnp.float32)
    row_squares = lax.psum(jnp.sum(floats * floats, axis=1), "width")
    normed = (
        floats * lax.rsqrt(row_squares / width_full + EPSILON)[:, None] * norm_gain[None, :]
    ).astype(jnp.bfloat16)
    query_cols = w_query.shape[1]
    kv_width = w_key.shape[1]
    weights_all = jnp.concatenate([w_query, w_key, w_value], axis=1)
    partial_sums = jnp.dot(
        lax.all_gather(normed, "blk", axis=0, tiled=True),
        weights_all,
        preferred_element_type=jnp.float32,
    )
    summed = lax.psum(partial_sums, "width")
    q_raw = summed[:, :query_cols]
    kv_raw = summed[:, query_cols:]
    query_rows = q_raw.shape[0]
    stacked = jnp.stack([kv_raw[:, :kv_width], kv_raw[:, kv_width:]])
    every_kv = lax.all_gather(stacked.astype(jnp.bfloat16), "blk", axis=2, tiled=True).astype(
        stacked.dtype
    )
    heads_dev = query_cols // HEAD
    group = HEADS // KV_HEADS
    kv_index = lax.axis_index("blk") * heads_dev // group
    split_heads = every_kv.reshape(2, total_rows, HEAD, KV_HEADS)
    own_head = lax.dynamic_index_in_dim(split_heads, kv_index, 3, keepdims=False)
    keys_raw = own_head[0]
    values_raw = own_head[1]
    index_row = jnp.arange(total_rows, dtype=jnp.int32)
    starts = jnp.sum((seq_ids[None, :] < seq_ids[:, None]).astype(jnp.int32), axis=1)
    positions = index_row - starts
    queries = rotate(q_raw.reshape(query_rows, heads_dev, HEAD), positions).astype(jnp.bfloat16)
    keys_rot = rotate(keys_raw[:, None, :], positions)[:, 0, :].astype(jnp.bfloat16)
    values_bf = values_raw.astype(jnp.bfloat16)
    scores = jnp.einsum(
        "thd,sd->hts", queries, keys_rot, preferred_element_type=jnp.float32
    ) / jnp.sqrt(jnp.float32(HEAD))
    allowed = (seq_ids[None, :] == seq_ids[:, None]) & (index_row[None, :] <= index_row[:, None])
    scores = jnp.where(allowed[None], scores, jnp.float32(-jnp.inf))
    row_top = jnp.max(scores, axis=-1, keepdims=True)
    raised = jnp.exp(scores - row_top)
    probs = (raised / jnp.sum(raised, axis=-1, keepdims=True)).astype(jnp.bfloat16)
    context = jnp.einsum("hts,sd->thd", probs, values_bf, preferred_element_type=jnp.float32)
    context = context.astype(jnp.bfloat16).reshape(query_rows, query_cols)
    complete = lax.psum(
        jnp.dot(context, w_output, preferred_element_type=jnp.float32).astype(jnp.bfloat16), "blk"
    ).astype(jnp.float32)
    result = lax.dynamic_slice_in_dim(complete, lax.axis_index("blk") * rows_blk, rows_blk, 0)
    return result.astype(jnp.bfloat16)


def fused_kernel(
    tok, gain, wq_hbm, wk_hbm, wv_hbm, wo_hbm, seq, out,
    wq, wkv, wo, xg, acc_q, acc_kv, acc_ss, q_send, q_recv, ss_send, ss_recv,
    kv_send, kv_recv, cos_q, sin_q, cos_k, sin_k, bias, ctx, part, y_part, summed, z_part,
    w_sem, wo_sem, kvw_sem, gz_send, gz_recv, gy_send, gy_recv,
    ex_send, ex_recv, kv_ssem, kv_rsem, ry_send, ry_recv, rz_send, rz_recv,
):
    rows, width = tok.shape
    n = NZ * NY
    total = rows * n
    cols = wq.shape[1]
    heads_dev = cols // HEAD
    kvw = wk_hbm.shape[0]
    per_head = kvw // KV_HEADS
    span = width // CHUNKS
    tile = min(TILE, span)
    half = HEAD // 2
    f32, bf16 = jnp.float32, jnp.bfloat16

    me = lax.axis_index("blk")
    core = lax.axis_index("width")
    y = me % NY
    z = me // NY
    other = 1 - core
    y_peer = z * NY + (1 - y)

    def chunk(c):
        return pl.ds(c * span, span)

    near = z // 2
    inner = (1 - near) * z + near * (NZ - 1 - z)
    inward = (z + 1 - 2 * near) * NY + y
    outward = (z - 1 + 2 * near) * NY + y

    def place(k):
        at = (inner, 1 - inner, 2, 3)[k]
        return (1 - near) * at + near * (NZ - 1 - at)

    wq_copies = [
        pltpu.make_async_copy(wq_hbm.at[chunk(c), :], wq.at[chunk(c), :], w_sem.at[c])
        for c in range(CHUNKS)
    ]
    wo_copies = [
        pltpu.make_async_copy(wo_hbm.at[:, chunk(c)], wo.at[:, chunk(c)], wo_sem.at[c])
        for c in range(CHUNKS)
    ]
    wk_copy = pltpu.make_async_copy(wk_hbm, wkv.at[0:kvw, :], kvw_sem.at[0])
    wv_copy = pltpu.make_async_copy(wv_hbm, wkv.at[kvw:2 * kvw, :], kvw_sem.at[1])
    wk_copy.start()
    wv_copy.start()
    for copy in wq_copies + wo_copies:
        copy.start()

    barrier = pltpu.get_barrier_semaphore()
    for step in range(n):
        for side in range(WIDTH):
            if step == 0 and side == 0:
                continue
            pl.semaphore_signal(
                barrier, inc=1,
                device_id={"blk": (me + step) % n, "width": (core + side) % WIDTH},
                device_id_type=pl.DeviceIdType.MESH,
            )
    pl.semaphore_wait(barrier, n * WIDTH - 1)

    def remote(src, dst, s_sem, r_sem, blk, side):
        return pltpu.make_async_remote_copy(
            src_ref=src, dst_ref=dst, send_sem=s_sem, recv_sem=r_sem,
            device_id={"blk": blk, "width": side}, device_id_type=pl.DeviceIdType.MESH,
        )

    def gz(src, c, k_src, k_dst, blk_from, to):
        return remote(src, xg.at[c, blk_from], gz_send.at[c, k_src], gz_recv.at[c, k_dst], to, core)

    def own_in(c):
        return gz(tok.at[:, chunk(c)], c, 0, 1 + inner, me, inward)

    def own_out(c):
        return gz(tok.at[:, chunk(c)], c, 1, 1, me, outward)

    def on_in(c):
        blk = place(1) * NY + y
        return gz(xg.at[c, blk], c, 2, 3, blk, inward)

    def on_out(c, k):
        blk = place(k) * NY + y
        return gz(xg.at[c, blk], c, k + 1, k, blk, outward)

    def gz_in(c, k):
        return gz(tok.at[:, chunk(c)], c, 0, k, place(k) * NY + y, inward)

    def gy(c, k):
        blk = place(k) * NY + y
        src = tok.at[:, chunk(c)] if k == 0 else xg.at[c, blk]
        return remote(src, xg.at[c, blk], gy_send.at[c, k], gy_recv.at[c, k], y_peer, core)

    def gy_in(c, k):
        blk = place(k) * NY + (1 - y)
        return remote(tok.at[:, chunk(c)], xg.at[c, blk], gy_send.at[c, k], gy_recv.at[c, k], y_peer, core)

    for c in range(CHUNKS):
        own_in(c).start()
        gy(c, 0).start()

        @pl.when(inner == 1)
        def _():
            own_out(c).start()

    for c in range(CHUNKS):
        xg[c, me] = tok[:, c * span:(c + 1) * span]
    acc_q[...] = jnp.zeros_like(acc_q)
    acc_kv[...] = jnp.zeros_like(acc_kv)
    acc_ss[...] = jnp.zeros_like(acc_ss)
    by_col = jnp.broadcast_to(seq[...].astype(f32), (total, total))
    by_row = by_col.T
    at_row = lax.broadcasted_iota(jnp.int32, (total, total), 0)
    at_col = lax.broadcasted_iota(jnp.int32, (total, total), 1)
    starts_q = jnp.sum((by_col < by_row).astype(f32), axis=1, keepdims=True)
    starts_k = jnp.sum((by_row < by_col).astype(f32), axis=0, keepdims=True)
    bias[...] = jnp.where((by_col == by_row) & (at_col <= at_row), 0.0, -jnp.inf).astype(f32)
    rate = -2.0 * math.log(THETA) / HEAD
    lane = lax.broadcasted_iota(jnp.int32, (total, HEAD), 1)
    line = lax.broadcasted_iota(jnp.int32, (total, HEAD), 0)
    angle_q = (line.astype(f32) - starts_q) * jnp.exp((lane % half).astype(f32) * rate)
    cos_q[...] = jnp.cos(angle_q)
    sine = jnp.sin(angle_q)
    sin_q[...] = jnp.where(lane < half, -sine, sine)
    pos_k = lax.broadcasted_iota(jnp.int32, (half, total), 1).astype(f32) - starts_k
    angle_k = pos_k * jnp.exp(lax.broadcasted_iota(jnp.int32, (half, total), 0).astype(f32) * rate)
    cos_k[...] = jnp.cos(angle_k)
    sin_k[...] = jnp.sin(angle_k)

    def pass_on(c, k):
        gz_in(c, k).wait_recv()

        @pl.when(inner == 1)
        def _():
            (on_in(c) if k == 1 else on_out(c, k)).start()

        gy(c, k).start()

    def project(c):
        def body(k, _):
            here = pl.ds(pl.multiple_of(k * tile, tile), tile)
            deep = pl.ds(pl.multiple_of(c * span + k * tile, tile), tile)
            x = xg[c, :, :, here].reshape(total, tile).astype(f32)
            squares = x * x
            folded = squares[:, :HEAD]
            for i in range(1, tile // HEAD):
                folded = folded + squares[:, i * HEAD:(i + 1) * HEAD]
            acc_ss[...] += folded
            scaled = (x * gain[:, deep]).astype(bf16)
            acc_q[...] += jnp.dot(scaled, wq[deep, :], preferred_element_type=f32)
            acc_kv[...] += lax.dot_general(wkv[:, deep], scaled, NT, preferred_element_type=f32)
            return 0

        lax.fori_loop(0, span // tile, body, 0)

    for k in range(1, NZ):
        for c in range(CHUNKS):
            pass_on(c, k)
    for c in range(CHUNKS):
        for k in range(NZ):
            gy_in(c, k).wait_recv()
        if c == 0:
            wk_copy.wait()
            wv_copy.wait()
        wq_copies[c].wait()
        project(c)

    rr = lax.broadcasted_iota(jnp.int32, (2 * kvw, 2 * kvw), 0)
    cc = lax.broadcasted_iota(jnp.int32, (2 * kvw, 2 * kvw), 1)
    at = ((rr // per_head) % 2) * kvw + (rr % per_head) * KV_HEADS + rr // (2 * per_head)
    picks = jnp.where(cc == at, 1.0, 0.0).astype(bf16)
    turned = jnp.dot(picks, acc_kv[...].astype(bf16), preferred_element_type=f32)
    kv_send[...] = turned.astype(bf16).reshape(KV_HEADS, 2 * per_head, total)
    group = HEADS // KV_HEADS

    def kv_copy(step, side, blk, whose):
        to = (me + step) % n
        i = step * WIDTH + side
        return remote(
            kv_send.at[to * heads_dev // group], kv_recv.at[whose, blk],
            kv_ssem.at[i], kv_rsem.at[i], to, (core + side) % WIDTH,
        )

    pairs = [(s, side) for s in range(n) for side in range(WIDTH) if s or side]
    for s, side in pairs:
        kv_copy(s, side, me, core).start()
    kv_recv[core, me] = kv_send[me * heads_dev // group]
    ss_send[...] = jnp.broadcast_to(jnp.sum(acc_ss[...], axis=1, keepdims=True), (total, HEAD))
    ss_copy = remote(ss_send, ss_recv, ex_send.at[0], ex_recv.at[0], me, other)
    ss_copy.start()
    q_send[...] = acc_q[...].astype(bf16)
    q_copy = remote(q_send, q_recv, ex_send.at[1], ex_recv.at[1], me, other)
    q_copy.start()

    ss_copy.wait_recv()
    scale = lax.rsqrt((ss_send[...] + ss_recv[...]) / (WIDTH * width) + EPSILON)
    scale_k = scale.T
    q_copy.wait_recv()
    for s, side in pairs:
        kv_copy(s, side, (me + n - s) % n, (core + side) % WIDTH).wait_recv()
    kv = kv_recv[0].astype(f32) + kv_recv[1].astype(f32)
    keys = kv[:, :per_head].reshape(HEAD, total) * scale_k
    values = (kv[:, per_head:].reshape(HEAD, total) * scale_k).astype(bf16)
    low, high = keys[:half], keys[half:]
    keys = jnp.concatenate(
        [low * cos_k[...] - high * sin_k[...], high * cos_k[...] + low * sin_k[...]], axis=0
    ).astype(bf16)
    for h in range(heads_dev):
        own = slice(h * HEAD, (h + 1) * HEAD)
        q = (acc_q[:, own] + q_recv[:, own].astype(f32)) * scale
        q = (q * cos_q[...] + pltpu.roll(q, half, 1) * sin_q[...]).astype(bf16)
        scores = jnp.dot(q, keys, preferred_element_type=f32) * (1.0 / math.sqrt(HEAD)) + bias[...]
        raised = jnp.exp(scores - jnp.max(scores, axis=1, keepdims=True))
        probs = (raised / jnp.sum(raised, axis=1, keepdims=True)).astype(bf16)
        ctx[:, own] = lax.dot_general(probs, values, NT, preferred_element_type=f32).astype(bf16)

    def ry(c, k):
        at = place(k)
        return remote(part.at[c, 1 - y, at], y_part.at[c, k], ry_send.at[c, k], ry_recv.at[c, k], y_peer, core)

    def rz(c, k, slot, to):
        return remote(summed.at[c, k], z_part.at[c, slot], rz_send.at[c, k], rz_recv.at[c, slot], to, core)

    END = {3: 3, 2: 2, 1: 0}
    MIDDLE = {3: 1, 2: 4, 1: 0}

    def rz_in(c, slot):
        return rz(c, 1, slot, inward)

    def multiply(c):
        wo_copies[c].wait()

        def body(k, _):
            here = pl.ds(pl.multiple_of(k * tile, tile), tile)
            deep = pl.ds(pl.multiple_of(c * span + k * tile, tile), tile)
            got = jnp.dot(ctx[...], wo[:, deep], preferred_element_type=f32).astype(bf16)
            got = got.reshape(NZ, NY, rows, tile)
            for i in range(NY):
                part[c, i, :, :, here] = got[:, i]
            return 0

        lax.fori_loop(0, span // tile, body, 0)
        for k in reversed(range(NZ)):
            ry(c, k).start()

    def reduce(c):
        for k in reversed(range(1, NZ)):
            ry(c, k).wait_recv()

            @pl.when(inner == 0)
            def _():
                summed[c, k] = (part[c, y, place(k)].astype(f32) + y_part[c, k].astype(f32)).astype(bf16)
                rz(c, k, END[k], inward).start()

            @pl.when(inner == 1)
            def _():
                rz_in(c, k).wait_recv()
                summed[c, k] = (
                    part[c, y, place(k)].astype(f32) + y_part[c, k].astype(f32) + z_part[c, k].astype(f32)
                ).astype(bf16)
                rz(c, k, MIDDLE[k], outward if k == 1 else inward).start()

    def finish(c):
        ry(c, 0).wait_recv()
        rz_in(c, 0).wait_recv()
        found = part[c, y, z].astype(f32) + y_part[c, 0].astype(f32) + z_part[c, 0].astype(f32)

        @pl.when(inner == 0)
        def _():
            out[:, c * span:(c + 1) * span] = found.astype(bf16)

        @pl.when(inner == 1)
        def _():
            rz_in(c, 4).wait_recv()
            out[:, c * span:(c + 1) * span] = (
                part[c, y, z].astype(f32) + y_part[c, 0].astype(f32)
                + z_part[c, 0].astype(f32) + z_part[c, 4].astype(f32)
            ).astype(bf16)

    for c in range(CHUNKS):
        multiply(c)
        if c > 0:
            reduce(c - 1)
    reduce(CHUNKS - 1)
    for c in range(CHUNKS):
        finish(c)

    for c in range(CHUNKS):
        own_in(c).wait_send()

        @pl.when(inner == 1)
        def _():
            own_out(c).wait_send()
            on_in(c).wait_send()
            for k in range(2, NZ):
                on_out(c, k).wait_send()

        for k in range(1, NZ):
            rz(c, k, 0, inward).wait_send()
        for k in range(NZ):
            gy(c, k).wait_send()
            ry(c, k).wait_send()
    for s, side in pairs:
        kv_copy(s, side, me, core).wait_send()
    ss_copy.wait_send()
    q_copy.wait_send()


def kernel_form(tokens, norm_gain, w_query, w_key, w_value, w_output, seq_ids):
    rows, width = tokens.shape
    n = NZ * NY
    total = rows * n
    cols = w_query.shape[1]
    kvw = w_key.shape[1]
    per_head = kvw // KV_HEADS
    span = width // CHUNKS
    bf16, f32 = jnp.bfloat16, jnp.float32
    vmem = pl.BlockSpec(memory_space=pltpu.VMEM)
    hbm = pl.BlockSpec(memory_space=pl.ANY)
    dma = pltpu.SemaphoreType.DMA
    return pl.pallas_call(
        fused_kernel,
        out_shape=jax.ShapeDtypeStruct((rows, width), bf16),
        in_specs=[vmem, vmem, hbm, hbm, hbm, hbm, vmem],
        out_specs=vmem,
        scratch_shapes=[
            pltpu.VMEM((width, cols), bf16),
            pltpu.VMEM((2 * kvw, width), bf16),
            pltpu.VMEM((cols, width), bf16),
            pltpu.VMEM((CHUNKS, n, rows, span), bf16),
            pltpu.VMEM((total, cols), f32),
            pltpu.VMEM((2 * kvw, total), f32),
            pltpu.VMEM((total, HEAD), f32),
            pltpu.VMEM((total, cols), bf16),
            pltpu.VMEM((total, cols), bf16),
            pltpu.VMEM((total, HEAD), f32),
            pltpu.VMEM((total, HEAD), f32),
            pltpu.VMEM((KV_HEADS, 2 * per_head, total), bf16),
            pltpu.VMEM((WIDTH, n, 2 * per_head, total), bf16),
            pltpu.VMEM((total, HEAD), f32),
            pltpu.VMEM((total, HEAD), f32),
            pltpu.VMEM((HEAD // 2, total), f32),
            pltpu.VMEM((HEAD // 2, total), f32),
            pltpu.VMEM((total, total), f32),
            pltpu.VMEM((total, cols), bf16),
            pltpu.VMEM((CHUNKS, NY, NZ, rows, span), bf16),
            pltpu.VMEM((CHUNKS, NZ, rows, span), bf16),
            pltpu.VMEM((CHUNKS, NZ, rows, span), bf16),
            pltpu.VMEM((CHUNKS, NZ + 1, rows, span), bf16),
            dma((CHUNKS,)),
            dma((CHUNKS,)),
            dma((2,)),
            dma((CHUNKS, NZ + 1)),
            dma((CHUNKS, NZ)),
            dma((CHUNKS, NZ)),
            dma((CHUNKS, NZ)),
            dma((2,)),
            dma((2,)),
            dma((n * WIDTH,)),
            dma((n * WIDTH,)),
            dma((CHUNKS, NZ)),
            dma((CHUNKS, NZ)),
            dma((CHUNKS, NZ)),
            dma((CHUNKS, NZ + 1)),
        ],
        compiler_params=pltpu.CompilerParams(
            collective_id=0, has_side_effects=True, vmem_limit_bytes=60 * 1024 * 1024
        ),
        name="attention_block",
    )(
        tokens, norm_gain.reshape(1, width), w_query, w_key.T, w_value.T, w_output,
        seq_ids.reshape(1, total),
    )


def solution(mesh):
    placed = (
        P(("rep", "blk"), "width"),
        P("width"),
        P("width", "blk"),
        P("width", "blk"),
        P("width", "blk"),
        P("blk", "width"),
        P("rep"),
    )
    on_grid = mesh.shape["blk"] == NZ * NY and mesh.shape["width"] == WIDTH
    return jax.shard_map(
        kernel_form if on_grid else collective_form,
        mesh=mesh, in_specs=placed, out_specs=P(("rep", "blk"), "width"), check_vma=False,
    )
```

```python
import functools
import math

import jax
import jax.numpy as jnp
from jax import lax
from jax.experimental import pallas as pl
from jax.experimental.pallas import tpu as pltpu
from jax.sharding import PartitionSpec as P

HEADS = 64
KV_HEADS = 4
HEAD = 128

EPSILON = 1e-05
THETA = 500000.0

NZ = 4
NY = 2
WIDTH = 2
CHUNKS = 4
TILE = 1024

NT = (((1,), (1,)), ((), ()))


def rotate(values_in, positions):
    half_dim = values_in.shape[-1] // 2
    freqs = THETA ** (-2.0 * jnp.arange(half_dim, dtype=jnp.float32) / values_in.shape[-1])
    angles = positions.astype(jnp.float32)[:, None] * freqs[None, :]
    cosine = jnp.cos(angles)[:, None, :]
    sine = jnp.sin(angles)[:, None, :]
    lower = values_in[..., :half_dim]
    upper = values_in[..., half_dim:]
    return jnp.concatenate([lower * cosine - upper * sine, upper * cosine + lower * sine], axis=-1)


def collective_form(tokens, norm_gain, w_query, w_key, w_value, w_output, seq_ids):
    rows_blk, half_width = tokens.shape
    width_full = half_width * lax.axis_size("width")
    total_rows = rows_blk * lax.axis_size("blk")
    floats = tokens.astype(jnp.float32)
    row_squares = lax.psum(jnp.sum(floats * floats, axis=1), "width")
    normed = (
        floats * lax.rsqrt(row_squares / width_full + EPSILON)[:, None] * norm_gain[None, :]
    ).astype(jnp.bfloat16)
    query_cols = w_query.shape[1]
    kv_width = w_key.shape[1]
    weights_all = jnp.concatenate([w_query, w_key, w_value], axis=1)
    partial_sums = jnp.dot(
        lax.all_gather(normed, "blk", axis=0, tiled=True),
        weights_all,
        preferred_element_type=jnp.float32,
    )
    summed = lax.psum(partial_sums, "width")
    q_raw = summed[:, :query_cols]
    kv_raw = summed[:, query_cols:]
    query_rows = q_raw.shape[0]
    stacked = jnp.stack([kv_raw[:, :kv_width], kv_raw[:, kv_width:]])
    every_kv = lax.all_gather(stacked.astype(jnp.bfloat16), "blk", axis=2, tiled=True).astype(
        stacked.dtype
    )
    heads_dev = query_cols // HEAD
    group = HEADS // KV_HEADS
    kv_index = lax.axis_index("blk") * heads_dev // group
    split_heads = every_kv.reshape(2, total_rows, HEAD, KV_HEADS)
    own_head = lax.dynamic_index_in_dim(split_heads, kv_index, 3, keepdims=False)
    keys_raw = own_head[0]
    values_raw = own_head[1]
    index_row = jnp.arange(total_rows, dtype=jnp.int32)
    starts = jnp.sum((seq_ids[None, :] < seq_ids[:, None]).astype(jnp.int32), axis=1)
    positions = index_row - starts
    queries = rotate(q_raw.reshape(query_rows, heads_dev, HEAD), positions).astype(jnp.bfloat16)
    keys_rot = rotate(keys_raw[:, None, :], positions)[:, 0, :].astype(jnp.bfloat16)
    values_bf = values_raw.astype(jnp.bfloat16)
    scores = jnp.einsum(
        "thd,sd->hts", queries, keys_rot, preferred_element_type=jnp.float32
    ) / jnp.sqrt(jnp.float32(HEAD))
    allowed = (seq_ids[None, :] == seq_ids[:, None]) & (index_row[None, :] <= index_row[:, None])
    scores = jnp.where(allowed[None], scores, jnp.float32(-jnp.inf))
    row_top = jnp.max(scores, axis=-1, keepdims=True)
    raised = jnp.exp(scores - row_top)
    probs = (raised / jnp.sum(raised, axis=-1, keepdims=True)).astype(jnp.bfloat16)
    context = jnp.einsum("hts,sd->thd", probs, values_bf, preferred_element_type=jnp.float32)
    context = context.astype(jnp.bfloat16).reshape(query_rows, query_cols)
    complete = lax.psum(
        jnp.dot(context, w_output, preferred_element_type=jnp.float32).astype(jnp.bfloat16), "blk"
    ).astype(jnp.float32)
    result = lax.dynamic_slice_in_dim(complete, lax.axis_index("blk") * rows_blk, rows_blk, 0)
    return result.astype(jnp.bfloat16)


def fused_kernel(
    tok, gain, wq_hbm, wk_hbm, wv_hbm, wo_hbm, seq, out,
    wq, wkv, wo, xg, acc_q, acc_kv, acc_ss, q_send, q_recv, ss_send, ss_recv,
    kv_send, kv_recv, cos_q, sin_q, cos_k, sin_k, bias, ctx, part, y_part, summed, z_part,
    w_sem, wo_sem, kvw_sem, gz_send, gz_recv, gy_send, gy_recv,
    ex_send, ex_recv, kv_ssem, kv_rsem, ry_send, ry_recv, rz_send, rz_recv,
):
    rows, width = tok.shape
    n = NZ * NY
    total = rows * n
    cols = wq.shape[1]
    heads_dev = cols // HEAD
    kvw = wk_hbm.shape[0]
    per_head = kvw // KV_HEADS
    span = width // CHUNKS
    tile = min(TILE, span)
    half = HEAD // 2
    f32, bf16 = jnp.float32, jnp.bfloat16

    me = lax.axis_index("blk")
    core = lax.axis_index("width")
    y = me % NY
    z = me // NY
    other = 1 - core
    y_peer = z * NY + (1 - y)

    def chunk(c):
        return pl.ds(c * span, span)

    near = z // 2
    inner = (1 - near) * z + near * (NZ - 1 - z)
    inward = (z + 1 - 2 * near) * NY + y
    outward = (z - 1 + 2 * near) * NY + y

    def place(k):
        at = (inner, 1 - inner, 2, 3)[k]
        return (1 - near) * at + near * (NZ - 1 - at)

    wq_copies = [
        pltpu.make_async_copy(wq_hbm.at[chunk(c), :], wq.at[chunk(c), :], w_sem.at[c])
        for c in range(CHUNKS)
    ]
    wo_copies = [
        pltpu.make_async_copy(wo_hbm.at[:, chunk(c)], wo.at[:, chunk(c)], wo_sem.at[c])
        for c in range(CHUNKS)
    ]
    wk_copy = pltpu.make_async_copy(wk_hbm, wkv.at[0:kvw, :], kvw_sem.at[0])
    wv_copy = pltpu.make_async_copy(wv_hbm, wkv.at[kvw:2 * kvw, :], kvw_sem.at[1])
    wk_copy.start()
    wv_copy.start()
    for copy in wq_copies + wo_copies:
        copy.start()

    barrier = pltpu.get_barrier_semaphore()
    for step in range(n):
        for side in range(WIDTH):
            if step == 0 and side == 0:
                continue
            pl.semaphore_signal(
                barrier, inc=1,
                device_id={"blk": (me + step) % n, "width": (core + side) % WIDTH},
                device_id_type=pl.DeviceIdType.MESH,
            )
    pl.semaphore_wait(barrier, n * WIDTH - 1)

    def remote(src, dst, s_sem, r_sem, blk, side):
        return pltpu.make_async_remote_copy(
            src_ref=src, dst_ref=dst, send_sem=s_sem, recv_sem=r_sem,
            device_id={"blk": blk, "width": side}, device_id_type=pl.DeviceIdType.MESH,
        )

    def gz(src, c, k_src, k_dst, blk_from, to):
        return remote(src, xg.at[c, blk_from], gz_send.at[c, k_src], gz_recv.at[c, k_dst], to, core)

    def own_in(c):
        return gz(tok.at[:, chunk(c)], c, 0, 1 + inner, me, inward)

    def own_out(c):
        return gz(tok.at[:, chunk(c)], c, 1, 1, me, outward)

    def on_in(c):
        blk = place(1) * NY + y
        return gz(xg.at[c, blk], c, 2, 3, blk, inward)

    def on_out(c, k):
        blk = place(k) * NY + y
        return gz(xg.at[c, blk], c, k + 1, k, blk, outward)

    def gz_in(c, k):
        return gz(tok.at[:, chunk(c)], c, 0, k, place(k) * NY + y, inward)

    def gy(c, k):
        blk = place(k) * NY + y
        src = tok.at[:, chunk(c)] if k == 0 else xg.at[c, blk]
        return remote(src, xg.at[c, blk], gy_send.at[c, k], gy_recv.at[c, k], y_peer, core)

    def gy_in(c, k):
        blk = place(k) * NY + (1 - y)
        return remote(tok.at[:, chunk(c)], xg.at[c, blk], gy_send.at[c, k], gy_recv.at[c, k], y_peer, core)

    for c in range(CHUNKS):
        own_in(c).start()
        gy(c, 0).start()

        @pl.when(inner == 1)
        def _():
            own_out(c).start()

    for c in range(CHUNKS):
        xg[c, me] = tok[:, c * span:(c + 1) * span]
    acc_q[...] = jnp.zeros_like(acc_q)
    acc_kv[...] = jnp.zeros_like(acc_kv)
    acc_ss[...] = jnp.zeros_like(acc_ss)
    by_col = jnp.broadcast_to(seq[...].astype(f32), (total, total))
    by_row = by_col.T
    at_row = lax.broadcasted_iota(jnp.int32, (total, total), 0)
    at_col = lax.broadcasted_iota(jnp.int32, (total, total), 1)
    starts_q = jnp.sum((by_col < by_row).astype(f32), axis=1, keepdims=True)
    starts_k = jnp.sum((by_row < by_col).astype(f32), axis=0, keepdims=True)
    bias[...] = jnp.where((by_col == by_row) & (at_col <= at_row), 0.0, -jnp.inf).astype(f32)
    rate = -2.0 * math.log(THETA) / HEAD
    lane = lax.broadcasted_iota(jnp.int32, (total, HEAD), 1)
    line = lax.broadcasted_iota(jnp.int32, (total, HEAD), 0)
    angle_q = (line.astype(f32) - starts_q) * jnp.exp((lane % half).astype(f32) * rate)
    cos_q[...] = jnp.cos(angle_q)
    sine = jnp.sin(angle_q)
    sin_q[...] = jnp.where(lane < half, -sine, sine)
    pos_k = lax.broadcasted_iota(jnp.int32, (half, total), 1).astype(f32) - starts_k
    angle_k = pos_k * jnp.exp(lax.broadcasted_iota(jnp.int32, (half, total), 0).astype(f32) * rate)
    cos_k[...] = jnp.cos(angle_k)
    sin_k[...] = jnp.sin(angle_k)

    def pass_on(c, k):
        gz_in(c, k).wait_recv()

        @pl.when(inner == 1)
        def _():
            (on_in(c) if k == 1 else on_out(c, k)).start()

        gy(c, k).start()

    def project(c):
        def body(k, _):
            here = pl.ds(pl.multiple_of(k * tile, tile), tile)
            deep = pl.ds(pl.multiple_of(c * span + k * tile, tile), tile)
            x = xg[c, :, :, here].reshape(total, tile).astype(f32)
            squares = x * x
            folded = squares[:, :HEAD]
            for i in range(1, tile // HEAD):
                folded = folded + squares[:, i * HEAD:(i + 1) * HEAD]
            acc_ss[...] += folded
            scaled = (x * gain[:, deep]).astype(bf16)
            acc_q[...] += jnp.dot(scaled, wq[deep, :], preferred_element_type=f32)
            acc_kv[...] += lax.dot_general(wkv[:, deep], scaled, NT, preferred_element_type=f32)
            return 0

        lax.fori_loop(0, span // tile, body, 0)

    for k in range(1, NZ):
        for c in range(CHUNKS):
            pass_on(c, k)
    for c in range(CHUNKS):
        for k in range(NZ):
            gy_in(c, k).wait_recv()
        if c == 0:
            wk_copy.wait()
            wv_copy.wait()
        wq_copies[c].wait()
        project(c)

    rr = lax.broadcasted_iota(jnp.int32, (2 * kvw, 2 * kvw), 0)
    cc = lax.broadcasted_iota(jnp.int32, (2 * kvw, 2 * kvw), 1)
    at = ((rr // per_head) % 2) * kvw + (rr % per_head) * KV_HEADS + rr // (2 * per_head)
    picks = jnp.where(cc == at, 1.0, 0.0).astype(bf16)
    turned = jnp.dot(picks, acc_kv[...].astype(bf16), preferred_element_type=f32)
    kv_send[...] = turned.astype(bf16).reshape(KV_HEADS, 2 * per_head, total)
    group = HEADS // KV_HEADS

    def kv_copy(step, side, blk, whose):
        to = (me + step) % n
        i = step * WIDTH + side
        return remote(
            kv_send.at[to * heads_dev // group], kv_recv.at[whose, blk],
            kv_ssem.at[i], kv_rsem.at[i], to, (core + side) % WIDTH,
        )

    pairs = [(s, side) for s in range(n) for side in range(WIDTH) if s or side]
    for s, side in pairs:
        kv_copy(s, side, me, core).start()
    kv_recv[core, me] = kv_send[me * heads_dev // group]
    ss_send[...] = jnp.broadcast_to(jnp.sum(acc_ss[...], axis=1, keepdims=True), (total, HEAD))
    ss_copy = remote(ss_send, ss_recv, ex_send.at[0], ex_recv.at[0], me, other)
    ss_copy.start()
    q_send[...] = acc_q[...].astype(bf16)
    q_copy = remote(q_send, q_recv, ex_send.at[1], ex_recv.at[1], me, other)
    q_copy.start()

    ss_copy.wait_recv()
    scale = lax.rsqrt((ss_send[...] + ss_recv[...]) / (WIDTH * width) + EPSILON)
    scale_k = scale.T
    q_copy.wait_recv()
    for s, side in pairs:
        kv_copy(s, side, (me + n - s) % n, (core + side) % WIDTH).wait_recv()
    kv = kv_recv[0].astype(f32) + kv_recv[1].astype(f32)
    keys = kv[:, :per_head].reshape(HEAD, total) * scale_k
    values = (kv[:, per_head:].reshape(HEAD, total) * scale_k).astype(bf16)
    low, high = keys[:half], keys[half:]
    keys = jnp.concatenate(
        [low * cos_k[...] - high * sin_k[...], high * cos_k[...] + low * sin_k[...]], axis=0
    ).astype(bf16)
    for h in range(heads_dev):
        own = slice(h * HEAD, (h + 1) * HEAD)
        q = (acc_q[:, own] + q_recv[:, own].astype(f32)) * scale
        q = (q * cos_q[...] + pltpu.roll(q, half, 1) * sin_q[...]).astype(bf16)
        scores = jnp.dot(q, keys, preferred_element_type=f32) * (1.0 / math.sqrt(HEAD)) + bias[...]
        raised = jnp.exp(scores - jnp.max(scores, axis=1, keepdims=True))
        probs = (raised / jnp.sum(raised, axis=1, keepdims=True)).astype(bf16)
        ctx[:, own] = lax.dot_general(probs, values, NT, preferred_element_type=f32).astype(bf16)

    def ry(c, k):
        at = place(k)
        return remote(part.at[c, 1 - y, at], y_part.at[c, k], ry_send.at[c, k], ry_recv.at[c, k], y_peer, core)

    def rz(c, k, slot, to):
        return remote(summed.at[c, k], z_part.at[c, slot], rz_send.at[c, k], rz_recv.at[c, slot], to, core)

    END = {3: 3, 2: 2, 1: 0}
    MIDDLE = {3: 1, 2: 4, 1: 0}

    def rz_in(c, slot):
        return rz(c, 1, slot, inward)

    def multiply(c):
        wo_copies[c].wait()

        def body(k, _):
            here = pl.ds(pl.multiple_of(k * tile, tile), tile)
            deep = pl.ds(pl.multiple_of(c * span + k * tile, tile), tile)
            got = jnp.dot(ctx[...], wo[:, deep], preferred_element_type=f32).astype(bf16)
            got = got.reshape(NZ, NY, rows, tile)
            for i in range(NY):
                part[c, i, :, :, here] = got[:, i]
            return 0

        lax.fori_loop(0, span // tile, body, 0)
        ry(c, NZ - 1).start()

    def reduce(c, k):
        if True:
            ry(c, k).wait_recv()

            @pl.when(inner == 0)
            def _():
                summed[c, k] = (part[c, y, place(k)].astype(f32) + y_part[c, k].astype(f32)).astype(bf16)
                rz(c, k, END[k], inward).start()

            @pl.when(inner == 1)
            def _():
                rz_in(c, k).wait_recv()
                summed[c, k] = (
                    part[c, y, place(k)].astype(f32) + y_part[c, k].astype(f32) + z_part[c, k].astype(f32)
                ).astype(bf16)
                rz(c, k, MIDDLE[k], outward if k == 1 else inward).start()

    def finish(c):
        ry(c, 0).wait_recv()
        rz_in(c, 0).wait_recv()
        found = part[c, y, z].astype(f32) + y_part[c, 0].astype(f32) + z_part[c, 0].astype(f32)

        @pl.when(inner == 0)
        def _():
            out[:, c * span:(c + 1) * span] = found.astype(bf16)

        @pl.when(inner == 1)
        def _():
            rz_in(c, 4).wait_recv()
            out[:, c * span:(c + 1) * span] = (
                part[c, y, z].astype(f32) + y_part[c, 0].astype(f32)
                + z_part[c, 0].astype(f32) + z_part[c, 4].astype(f32)
            ).astype(bf16)

    for c in range(CHUNKS):
        multiply(c)
    for k in reversed(range(NZ - 1)):
        for c in range(CHUNKS):
            ry(c, k).start()
    for k in reversed(range(1, NZ)):
        for c in range(CHUNKS):
            reduce(c, k)
    for c in range(CHUNKS):
        finish(c)

    for c in range(CHUNKS):
        own_in(c).wait_send()

        @pl.when(inner == 1)
        def _():
            own_out(c).wait_send()
            on_in(c).wait_send()
            for k in range(2, NZ):
                on_out(c, k).wait_send()

        for k in range(1, NZ):
            rz(c, k, 0, inward).wait_send()
        for k in range(NZ):
            gy(c, k).wait_send()
            ry(c, k).wait_send()
    for s, side in pairs:
        kv_copy(s, side, me, core).wait_send()
    ss_copy.wait_send()
    q_copy.wait_send()


def kernel_form(tokens, norm_gain, w_query, w_key, w_value, w_output, seq_ids):
    rows, width = tokens.shape
    n = NZ * NY
    total = rows * n
    cols = w_query.shape[1]
    kvw = w_key.shape[1]
    per_head = kvw // KV_HEADS
    span = width // CHUNKS
    bf16, f32 = jnp.bfloat16, jnp.float32
    vmem = pl.BlockSpec(memory_space=pltpu.VMEM)
    hbm = pl.BlockSpec(memory_space=pl.ANY)
    dma = pltpu.SemaphoreType.DMA
    return pl.pallas_call(
        fused_kernel,
        out_shape=jax.ShapeDtypeStruct((rows, width), bf16),
        in_specs=[vmem, vmem, hbm, hbm, hbm, hbm, vmem],
        out_specs=vmem,
        scratch_shapes=[
            pltpu.VMEM((width, cols), bf16),
            pltpu.VMEM((2 * kvw, width), bf16),
            pltpu.VMEM((cols, width), bf16),
            pltpu.VMEM((CHUNKS, n, rows, span), bf16),
            pltpu.VMEM((total, cols), f32),
            pltpu.VMEM((2 * kvw, total), f32),
            pltpu.VMEM((total, HEAD), f32),
            pltpu.VMEM((total, cols), bf16),
            pltpu.VMEM((total, cols), bf16),
            pltpu.VMEM((total, HEAD), f32),
            pltpu.VMEM((total, HEAD), f32),
            pltpu.VMEM((KV_HEADS, 2 * per_head, total), bf16),
            pltpu.VMEM((WIDTH, n, 2 * per_head, total), bf16),
            pltpu.VMEM((total, HEAD), f32),
            pltpu.VMEM((total, HEAD), f32),
            pltpu.VMEM((HEAD // 2, total), f32),
            pltpu.VMEM((HEAD // 2, total), f32),
            pltpu.VMEM((total, total), f32),
            pltpu.VMEM((total, cols), bf16),
            pltpu.VMEM((CHUNKS, NY, NZ, rows, span), bf16),
            pltpu.VMEM((CHUNKS, NZ, rows, span), bf16),
            pltpu.VMEM((CHUNKS, NZ, rows, span), bf16),
            pltpu.VMEM((CHUNKS, NZ + 1, rows, span), bf16),
            dma((CHUNKS,)),
            dma((CHUNKS,)),
            dma((2,)),
            dma((CHUNKS, NZ + 1)),
            dma((CHUNKS, NZ)),
            dma((CHUNKS, NZ)),
            dma((CHUNKS, NZ)),
            dma((2,)),
            dma((2,)),
            dma((n * WIDTH,)),
            dma((n * WIDTH,)),
            dma((CHUNKS, NZ)),
            dma((CHUNKS, NZ)),
            dma((CHUNKS, NZ)),
            dma((CHUNKS, NZ + 1)),
        ],
        compiler_params=pltpu.CompilerParams(
            collective_id=0, has_side_effects=True, vmem_limit_bytes=60 * 1024 * 1024
        ),
        name="attention_block",
    )(
        tokens, norm_gain.reshape(1, width), w_query, w_key.T, w_value.T, w_output,
        seq_ids.reshape(1, total),
    )


def solution(mesh):
    placed = (
        P(("rep", "blk"), "width"),
        P("width"),
        P("width", "blk"),
        P("width", "blk"),
        P("width", "blk"),
        P("blk", "width"),
        P("rep"),
    )
    on_grid = mesh.shape["blk"] == NZ * NY and mesh.shape["width"] == WIDTH
    return jax.shard_map(
        kernel_form if on_grid else collective_form,
        mesh=mesh, in_specs=placed, out_specs=P(("rep", "blk"), "width"), check_vma=False,
    )
```
